512 devices in a mesh: section: 16 (over y, x_lo), expert: 32 (over z, x_hi, core).
Axes of the slice: x: 4 (x_hi: 2, x_lo: 2; x = x_hi * 2 + x_lo), y: 8, z: 8, core: 2. Of those that a mesh axis runs over, the one named last changes fastest.
Arguments:
- left_x: bfloat16 [16, 2048, 3584], P('section', 'expert'), may hold values from -6 to 6
- left_cot: bfloat16 [16, 2048, 3584], P('section', 'expert'), may hold values from -6 to 6
- left_experts: int32 [16, 2048, 8], P('section', 'expert'), may hold values from 0 to 127, all different within a row; in each aligned block of 64 rows (0 to 63, 64 to 127, ..., all dimensions but the last counted through in order) at most 6 rows name the same one
- left_gates: float32 [16, 2048, 8], P('section', 'expert'), may hold values from 0.1 to 1
- right_x: bfloat16 [16, 2048, 3584], P('section', 'expert'), may hold values from -6 to 6
- right_cot: bfloat16 [16, 2048, 3584], P('section', 'expert'), may hold values from -6 to 6
- right_experts: int32 [16, 2048, 8], P('section', 'expert'), may hold values from 0 to 127, all different within a row; in each aligned block of 64 rows (0 to 63, 64 to 127, ..., all dimensions but the last counted through in order) at most 6 rows name the same one
- right_gates: float32 [16, 2048, 8], P('section', 'expert'), may hold values from 0.1 to 1
- up_weight: bfloat16 [16, 3584, 2048], P('section', None, 'expert'), may hold values from -0.09375 to 0.09375
- down_weight: bfloat16 [16, 3584, 2048], P('section', None, 'expert'), may hold values from -0.1875 to 0.1875
Outputs:
- left_grad_in: bfloat16 [16, 2048, 3584], P('section', 'expert')
- right_grad_in: bfloat16 [16, 2048, 3584], P('section', 'expert')
- layer_grad: bfloat16 [16, 3584, 4096], P('section', None, 'expert')
The draws below stay inside these ranges and needn't reach their ends.
Inputs may be any that keep to these rules, and one draw needn't show every extreme that they name: `left_experts`: in each device's 64 tokens no expert is named by more than 6 assignments, a bound that some block reaches; a token's 8 experts differ. `right_experts`: as for left_experts.
All inputs are finite; a program needn't handle non-finite values.
Results may differ from the reference program's by a relative error of at most 0.013.
Values may be sent and summed in bfloat16 or wider, within the bound.
No kernel may reach another device: no remote copies, remote signals or barrier semaphores. Data moves between devices by JAX's collectives and lax.ppermute only.
A program may use at most 64 MiB of HBM per device.

```python
import math
import jax
import jax.numpy as jnp
import numpy as np
from jax import lax

D = 3584
H = 1024
EXP_ALL = 128
EXPERTS = 2
TOPK = 8
TOK_DEV = 64
CAP = 6
SECTIONS = 16
TOK = 2048
N_EXPERT = 32


def steps_of(own_key, extent, shards, smallest, largest):
    level = 1.0
    for dim, parts in shards:
        steps = jax.random.uniform(jax.random.fold_in(jax.random.fold_in(own_key, 6), dim), (parts,), jnp.float32, smallest / len(shards), largest / len(shards))
        level = level * jnp.repeat(jnp.exp(steps), extent[dim] // parts).reshape((-1,) + (1,) * (len(extent) - 1 - dim))
    return level


def deal_out(own_key, own, number, rows, count, top, reach, skew):
    ranking = jax.random.permutation(own_key, count)
    heavy_load, usual = shares(count, rows * top, reach, skew, True), shares(count, rows * top, reach, skew, False)
    places = jnp.arange(count)

    def named(lengths, rotation):
        used = int((lengths > 0).sum())
        fixed = max(1, used // 4)
        moved = fixed + (places - fixed + rotation * (used - fixed)) % max(1, count - fixed)
        return jnp.zeros((count,), jnp.int32).at[ranking[jnp.where(places < fixed, places, moved)]].set(jnp.asarray(lengths, jnp.int32))

    lengths = jnp.where(number % 4 == 0, named(heavy_load, number // 4), named(usual, number - number // 4 - 1))
    mixed = jax.random.permutation(jax.random.fold_in(own, 3), count)
    giver, sink = mixed[0:count // 2 * 2:2], mixed[1:count // 2 * 2:2]
    margin = jnp.minimum(lengths[giver] - 1, reach - lengths[sink]) // 2
    margin = jnp.where((giver == ranking[0]) | (sink == ranking[0]) | (lengths[sink] == 0), 0, jnp.maximum(margin, 0))
    moved = jax.random.randint(jax.random.fold_in(own, 4), (count // 2,), 0, 1 << 20) % (margin + 1)
    lengths = lengths.at[giver].add(-moved).at[sink].add(moved)
    labels = jnp.searchsorted(jnp.cumsum(lengths), jnp.arange(rows * top), side="right").astype(jnp.int32)
    listing = labels.reshape(top, rows).T
    listing = listing[jax.random.permutation(jax.random.fold_in(own, 1), rows)]
    rotation = jax.random.randint(jax.random.fold_in(own, 2), (rows, 1), 0, top)
    return jnp.take_along_axis(listing, (jnp.arange(top)[None, :] + rotation) % top, axis=1)


def shares(count, total, bound, lean, full):
    weights = [(1 << 20) // math.isqrt(rank ** lean) + 1 for rank in range(1, count + 1)]
    largest = bound if full else min(bound, max(-(-total // count), total * weights[0] // sum(weights)))
    least = 1 if total - largest >= count - 1 else 0
    holding, surplus = [largest] + [least] * (count - 1), total - largest - least * (count - 1)
    while surplus > 0:
        candidates = [i for i in range(1, count) if holding[i] < largest] or [i for i in range(1, count) if holding[i] < bound]
        mass, remaining = sum([weights[i] for i in candidates]), surplus
        for i in candidates:
            extra = min(bound - holding[i], max(1, remaining * weights[i] // mass), surplus)
            holding[i] = holding[i] + extra
            surplus = surplus - extra
    return np.array(holding)


def gaussian(own_key, shape, width, reach, pieces=(), held_as=jnp.bfloat16):
    entries = width * jax.random.normal(own_key, shape, jnp.float32)
    if pieces:
        entries = entries * steps_of(own_key, shape, pieces, -0.22, 0.18)
    return jnp.clip(entries, -reach, reach).astype(held_as)


def setup_inputs(seed: int = 0) -> dict:
    key_list = jax.random.split(jax.random.key(seed), 11)
    left_x = gaussian(key_list[0], (SECTIONS, TOK, D), 1.0, 6.0, ((0, 16), (1, 32)))
    left_cot = gaussian(key_list[1], (SECTIONS, TOK, D), 1.0, 6.0, ((0, 16), (1, 32)))
    left_experts_keys = jax.random.split(jax.random.fold_in(key_list[2], 1), SECTIONS * TOK // TOK_DEV)
    left_experts_turns = jax.random.permutation(jax.random.fold_in(key_list[2], 3), SECTIONS * TOK // TOK_DEV)
    left_experts = jax.vmap(lambda own, number: deal_out(jax.random.fold_in(key_list[2], 2), own, number, TOK_DEV, EXP_ALL, TOPK, CAP, 2))(left_experts_keys, left_experts_turns).reshape((SECTIONS, TOK, TOPK))
    left_gates = jnp.clip(0.1 + 0.9 * jax.random.uniform(key_list[3], (SECTIONS, TOK, TOPK), jnp.float32) ** steps_of(key_list[3], (SECTIONS, TOK, TOPK), ((0, 16), (1, 32)), -0.2, 0.2), 0.1, 1.0)
    right_x = gaussian(key_list[4], (SECTIONS, TOK, D), 1.0, 6.0, ((0, 16), (1, 32)))
    right_cot = gaussian(key_list[5], (SECTIONS, TOK, D), 1.0, 6.0, ((0, 16), (1, 32)))
    right_experts_keys = jax.random.split(jax.random.fold_in(key_list[6], 1), SECTIONS * TOK // TOK_DEV)
    right_experts_turns = jax.random.permutation(jax.random.fold_in(key_list[6], 3), SECTIONS * TOK // TOK_DEV)
    right_experts = jax.vmap(lambda own, number: deal_out(jax.random.fold_in(key_list[6], 2), own, number, TOK_DEV, EXP_ALL, TOPK, CAP, 2))(right_experts_keys, right_experts_turns).reshape((SECTIONS, TOK, TOPK))
    right_gates = jnp.clip(0.1 + 0.9 * jax.random.uniform(key_list[7], (SECTIONS, TOK, TOPK), jnp.float32) ** steps_of(key_list[7], (SECTIONS, TOK, TOPK), ((0, 16), (1, 32)), -0.2, 0.2), 0.1, 1.0)
    up_weight = gaussian(key_list[8], (SECTIONS, D, EXPERTS * H), D ** -0.5, 0.09375, ((0, 16), (2, 32)))
    down_weight = gaussian(key_list[9], (SECTIONS, D, EXPERTS * H), H ** -0.5, 0.1875, ((0, 16), (2, 32)))
    return {"left_x": left_x, "left_cot": left_cot, "left_experts": left_experts, "left_gates": left_gates, "right_x": right_x, "right_cot": right_cot, "right_experts": right_experts, "right_gates": right_gates, "up_weight": up_weight, "down_weight": down_weight}


def slot_tables(experts, gates, n_exp, cap):
    tok, top = experts.shape
    flat = experts.reshape(-1)
    onehot = (flat[:, None] == jnp.arange(n_exp, dtype=jnp.int32)[None, :]).astype(jnp.int32)
    earlier = jnp.cumsum(onehot, axis=0) - onehot
    rank = jnp.sum(earlier * onehot, axis=1)
    position = (flat * cap + rank).reshape(tok, top)
    slots = jnp.arange(n_exp * cap, dtype=jnp.int32)
    hit = position[None, :, :] == slots[:, None, None]
    placed = jnp.sum(hit.astype(jnp.float32), axis=2)
    weighted = jnp.sum(jnp.where(hit, gates[None, :, :], jnp.float32(0.0)), axis=2)
    return placed, weighted


def section_backward(args):
    x, cot, experts, gates, up, down = args
    blocks = N_EXPERT
    groups = N_EXPERT // EXPERTS
    part = H // groups
    x_b = x.reshape(blocks, TOK_DEV, D).astype(jnp.float32)
    c_b = cot.reshape(blocks, TOK_DEV, D).astype(jnp.float32)
    placed, weighted = jax.vmap(lambda e, g: slot_tables(e, g, EXPERTS, CAP))(
        experts.reshape(blocks, TOK_DEV, TOPK), gates.reshape(blocks, TOK_DEV, TOPK))
    sent_x = jnp.einsum('bst,btd->bsd', placed, x_b, precision=lax.Precision.HIGHEST).astype(jnp.bfloat16)
    sent_g = jnp.einsum('bst,btd->bsd', weighted, c_b, precision=lax.Precision.HIGHEST).astype(jnp.bfloat16)
    ex = sent_x.reshape(blocks, EXPERTS, CAP, D).transpose(1, 0, 2, 3).reshape(EXPERTS, blocks * CAP, D).astype(jnp.float32)
    eg = sent_g.reshape(blocks, EXPERTS, CAP, D).transpose(1, 0, 2, 3).reshape(EXPERTS, blocks * CAP, D).astype(jnp.float32)
    wide_u = up.astype(jnp.float32).reshape(D, EXPERTS, H).transpose(1, 0, 2)
    wide_d = down.astype(jnp.float32).reshape(D, EXPERTS, H).transpose(1, 0, 2)
    act = jnp.einsum('erd,edh->erh', ex, wide_u)
    sig = jax.nn.sigmoid(act)
    hid = (act * sig).astype(jnp.bfloat16).astype(jnp.float32)
    back_h = jnp.einsum('erd,edh->erh', eg, wide_d)
    d_act = (back_h * sig * (1.0 + act * (1.0 - sig))).astype(jnp.bfloat16).astype(jnp.float32)
    grad_u = jnp.einsum('erd,erh->edh', ex, d_act).reshape(EXPERTS, D, groups, part)
    grad_d = jnp.einsum('erd,erh->edh', eg, hid).reshape(EXPERTS, D, groups, part)
    grad = jnp.concatenate([grad_u, grad_d], -1).transpose(1, 0, 2, 3).reshape(D, 2 * EXPERTS * H).astype(jnp.bfloat16)
    rows = blocks * CAP
    d_parts = jnp.einsum('erga,edga->egrd', d_act.reshape(EXPERTS, rows, groups, part), wide_u.reshape(EXPERTS, D, groups, part))
    d_slots = jnp.sum(d_parts.astype(jnp.bfloat16).astype(jnp.float32), axis=1)
    back = d_slots.reshape(EXPERTS, blocks, CAP, D).transpose(1, 0, 2, 3).reshape(blocks, EXPERTS * CAP, D)
    d_x = c_b + jnp.einsum('bst,bsd->btd', placed, back, precision=lax.Precision.HIGHEST)
    return d_x.reshape(TOK, D).astype(jnp.bfloat16), grad


def reference(left_x, left_cot, left_experts, left_gates, right_x, right_cot, right_experts, right_gates, up_weight, down_weight):
    dx_left, grad_left = lax.map(section_backward, (left_x, left_cot, left_experts, left_gates, up_weight, down_weight))
    dx_right, grad_right = lax.map(section_backward, (right_x, right_cot, right_experts, right_gates, up_weight[::-1], down_weight[::-1]))
    zero = jnp.zeros_like(dx_left[:1])
    left_grad_in = jnp.concatenate([dx_left[1:], zero], 0)
    right_grad_in = jnp.concatenate([zero, dx_right[:-1]], 0)
    layer_grad = (grad_left.astype(jnp.float32) + grad_right[::-1].astype(jnp.float32)).astype(jnp.bfloat16)
    return left_grad_in, right_grad_in, layer_grad
```

```python
import jax
import jax.numpy as jnp
from jax import lax
from jax.sharding import PartitionSpec as P

EXPERTS = 2
CAP = 6
BOTH = ("section", "expert")


def send(value, axis, route):
    size = lax.axis_size(axis)
    pairs = [(i, route(i)) for i in range(size)]
    return lax.ppermute(value, axis, [(a, b) for a, b in pairs if 0 <= b < size])


def slot_table(experts, order):
    hit = (experts[:, :, None] == order[None, None, :]).astype(jnp.float32)
    named = jnp.sum(hit, axis=1)
    rank = jnp.cumsum(named, axis=0) - named
    slots = jnp.arange(CAP, dtype=jnp.float32)
    table = named[:, :, None] * (rank[:, :, None] == slots).astype(jnp.float32)
    return hit, table


def dispatch(tokens, cot, experts, gates, order):
    half = tokens.shape[1] // 2
    hit, table = slot_table(experts, order)
    gate = jnp.sum(hit * gates[:, :, None], axis=1)
    slot_gate = jnp.sum(table * gate[:, :, None], axis=0)
    pick = table.astype(jnp.bfloat16)
    xs = jnp.einsum("ter,td->erd", pick, tokens, preferred_element_type=jnp.float32)
    cs = jnp.einsum("ter,td->erd", pick, cot, preferred_element_type=jnp.float32)
    xs = xs.astype(jnp.bfloat16)
    gs = (cs * slot_gate[:, :, None]).astype(jnp.bfloat16)
    kinds = [xs[..., :half], gs[..., :half], xs[..., half:], gs[..., half:]]
    return jnp.stack(kinds, axis=1)


def on_device(
    left_x,
    left_cot,
    left_experts,
    left_gates,
    right_x,
    right_cot,
    right_experts,
    right_gates,
    up_weight,
    down_weight,
):
    n_sec = lax.axis_size("section")
    n_exp = lax.axis_size("expert")
    groups = n_exp // EXPERTS
    width = left_x.shape[2]
    half = width // 2
    part = up_weight.shape[2]
    place = lax.axis_index("expert")
    own = place // groups
    core = place % 2
    order = jnp.stack([own, 1 - own]).astype(jnp.int32)

    left = dispatch(left_x[0], left_cot[0], left_experts[0], left_gates[0], order)
    right = dispatch(right_x[0], right_cot[0], right_experts[0], right_gates[0], order)

    def far(i):
        return (n_sec - 1 - i // n_exp) * n_exp + (i % n_exp + groups) % n_exp

    left_far = send(left[1], "expert", lambda j: (j + groups) % n_exp)
    right_near = send(right[0], "section", lambda s: n_sec - 1 - s)
    right_far = send(right[1], BOTH, far)

    next_cot = send(left_cot[0], "section", lambda s: s - 1)
    last_cot = send(right_cot[0], "section", lambda s: s + 1)
    next_experts = send(left_experts[0], "section", lambda s: s - 1)
    last_experts = send(right_experts[0], "section", lambda s: s + 1)

    shard = jnp.stack([left[0], right_near, left_far, right_far], axis=1)
    shard = shard.reshape(16 * CAP, half)
    same = [list(range(e * groups, (e + 1) * groups)) for e in range(EXPERTS)]
    rows = lax.all_gather(shard, "expert", axis=0, tiled=True, axis_index_groups=same)

    up, down = up_weight[0], down_weight[0]
    weights = jnp.concatenate([up[:half], down[:half], up[half:], down[half:]], axis=1)
    both = jnp.dot(rows, weights, preferred_element_type=jnp.float32)
    both = both.reshape(groups, 4, 4 * CAP, 4 * part)
    act = both[:, 0, :, :part] + both[:, 2, :, 2 * part : 3 * part]
    back_h = both[:, 1, :, part : 2 * part] + both[:, 3, :, 3 * part :]
    sig = jax.nn.sigmoid(act)
    hid = (act * sig).astype(jnp.bfloat16)
    d_act = (back_h * sig * (1.0 + act * (1.0 - sig))).astype(jnp.bfloat16)
    none = jnp.zeros_like(hid)
    spread = jnp.stack(
        [
            jnp.concatenate([d_act, none, none, none], axis=2),
            jnp.concatenate([none, hid, none, none], axis=2),
            jnp.concatenate([none, none, d_act, none], axis=2),
            jnp.concatenate([none, none, none, hid], axis=2),
        ],
        axis=1,
    ).reshape(groups * 16 * CAP, 4 * part)
    grad = lax.dot_general(
        rows, spread, (((0,), (0,)), ((), ())), preferred_element_type=jnp.float32
    ).astype(jnp.bfloat16)
    grad = jnp.concatenate([grad[:, : 2 * part], grad[:, 2 * part :]], axis=0)

    slots = lax.dot_general(
        d_act.reshape(-1, part), up, (((1,), (1,)), ((), ())), preferred_element_type=jnp.float32
    ).astype(jnp.bfloat16)
    slots = slots.reshape(groups // 2, 2, 4 * CAP, width)
    kept = lax.dynamic_index_in_dim(slots, core, 1, keepdims=False)
    given = lax.dynamic_index_in_dim(slots, 1 - core, 1, keepdims=False)
    got = send(given, "expert", lambda j: j ^ 1)
    summed = (kept.astype(jnp.float32) + got.astype(jnp.float32)).astype(jnp.bfloat16)
    summed = summed.reshape(groups // 2, 2, 2 * CAP, 2, half).transpose(1, 0, 3, 2, 4)
    summed = jnp.where(own == 0, summed, summed[::-1])
    summed = summed.reshape(groups * 4 * CAP, half)
    cores = [list(range(c, n_exp, 2)) for c in range(2)]
    back = lax.all_to_all(
        summed, "expert", split_axis=0, concat_axis=0, tiled=True, axis_index_groups=cores
    )
    back = back.reshape(EXPERTS, groups // 2, 2, 2, CAP, half).astype(jnp.float32)
    back = jnp.sum(back, axis=1).astype(jnp.bfloat16)
    back = back.transpose(2, 0, 3, 1, 4).reshape(2, EXPERTS * CAP, width)

    next_slots = send(back[0], "section", lambda s: s - 1)
    last_slots = send(back[1], "section", lambda s: n_sec - s)

    def finish(cot, experts, slots):
        _, table = slot_table(experts, jnp.arange(EXPERTS, dtype=jnp.int32))
        table = table.reshape(-1, EXPERTS * CAP).astype(jnp.bfloat16)
        added = jnp.dot(table, slots, preferred_element_type=jnp.float32)
        return (cot.astype(jnp.float32) + added).astype(jnp.bfloat16)[None]

    left_grad_in = finish(next_cot, next_experts, next_slots)
    right_grad_in = finish(last_cot, last_experts, last_slots)
    return left_grad_in, right_grad_in, grad[None]


def solution(mesh):
    return jax.shard_map(
        on_device,
        mesh=mesh,
        in_specs=(
            P("section", "expert", None),
            P("section", "expert", None),
            P("section", "expert", None),
            P("section", "expert", None),
            P("section", "expert", None),
            P("section", "expert", None),
            P("section", "expert", None),
            P("section", "expert", None),
            P("section", None, "expert"),
            P("section", None, "expert"),
        ),
        out_specs=(
            P("section", "expert", None),
            P("section", "expert", None),
            P("section", None, "expert"),
        ),
        check_vma=False,
    )
```

```python
import functools

import jax
import jax.numpy as jnp
from jax import lax
from jax.experimental import pallas as pl
from jax.experimental.pallas import tpu as pltpu
from jax.sharding import PartitionSpec as P

EXPERTS = 2
CAP = 6
KINDS = 4
NEAR = 4
RING = 8
BLOCK = KINDS * CAP
ROWS = RING * BLOCK
KIND_ROWS = RING * CAP
VMEM = pl.BlockSpec(memory_space=pltpu.VMEM)
SMEM = pl.BlockSpec(memory_space=pltpu.SMEM)
PARAMS = pltpu.CompilerParams(vmem_limit_bytes=48 * 1024 * 1024)


def send(value, axis, route):
    size = lax.axis_size(axis)
    pairs = [(i, route(i)) for i in range(size)]
    return lax.ppermute(value, axis, [(a, b) for a, b in pairs if 0 <= b < size])


def iota(shape, dim):
    return lax.broadcasted_iota(jnp.int32, shape, dim)


def nn(a, b):
    return jnp.dot(a, b, preferred_element_type=jnp.float32)


def nt(a, b):
    return lax.dot_general(a, b, (((1,), (1,)), ((), ())), preferred_element_type=jnp.float32)


def tn(a, b):
    return lax.dot_general(a, b, (((0,), (0,)), ((), ())), preferred_element_type=jnp.float32)


def one_hot(mask):
    return jnp.where(mask, 1.0, 0.0).astype(jnp.bfloat16)


def slot_table(experts, expert_of, slot_of):
    tokens = experts.shape[1]
    named = [
        jnp.sum(jnp.where(experts == e, 1.0, 0.0), axis=0, keepdims=True) for e in range(EXPERTS)
    ]
    named = jnp.where(expert_of == 0, named[0], named[1])
    before = one_hot(iota((tokens, tokens), 0) < iota((tokens, tokens), 1))
    rank = nn(named.astype(jnp.bfloat16), before)
    return jnp.where(rank == slot_of.astype(jnp.float32), named, 0.0)


def prepare_kernel(copies, x_ref, c_ref, e_ref, g_ref, o_ref):
    half = x_ref.shape[1] // 2
    experts, gates = e_ref[...], g_ref[...]
    shape = (EXPERTS * BLOCK, experts.shape[1])
    row = iota(shape, 0)
    expert_of, kind, slot_of = row // BLOCK, (row // CAP) % KINDS, row % CAP
    table = slot_table(experts, expert_of, slot_of)
    gate = [
        jnp.sum(jnp.where(experts == e, gates, 0.0), axis=0, keepdims=True) for e in range(EXPERTS)
    ]
    gate = jnp.sum(table * jnp.where(expert_of == 0, gate[0], gate[1]), axis=1, keepdims=True)
    scale = jnp.where(kind[:, :1] % 2 == 1, gate, 1.0)
    total = None
    sources = (x_ref[:, :half], c_ref[:, :half], x_ref[:, half:], c_ref[:, half:])
    for k, source in enumerate(sources):
        part = nn(jnp.where(kind == k, table, 0.0).astype(jnp.bfloat16), source)
        total = part if total is None else total + part
    out = (total * scale).astype(jnp.bfloat16)
    if copies == 1:
        o_ref[...] = out
    else:
        for e in range(EXPERTS):
            one = (total[e * BLOCK : (e + 1) * BLOCK] * scale[e * BLOCK : (e + 1) * BLOCK]).astype(
                jnp.bfloat16
            )
            two = jnp.concatenate([one, one], axis=0)
            for i in range(copies // 2):
                start = (e * copies + 2 * i) * BLOCK
                o_ref[start : start + 2 * BLOCK, :] = two


def prepare(x, cot, experts, gates, copies):
    return pl.pallas_call(
        functools.partial(prepare_kernel, copies),
        out_shape=jax.ShapeDtypeStruct((EXPERTS * copies * BLOCK, x.shape[1] // 2), jnp.bfloat16),
        in_specs=[VMEM] * 4,
        out_specs=VMEM,
        compiler_params=PARAMS,
        name="prepare",
    )(x, cot, experts, gates)


def work(rows, weights, aligned_ref, da_ref, hid_ref):
    half = rows.shape[1]
    part = weights.shape[0] // (2 * NEAR)
    out, src = iota((ROWS, ROWS), 0), iota((ROWS, ROWS), 1)
    within = out % KIND_ROWS
    wanted = (within // CAP) * BLOCK + (out // KIND_ROWS) * CAP + out % CAP
    aligned = nn(one_hot(src == wanted), rows).astype(jnp.bfloat16)
    aligned_ref[...] = aligned
    x0, g0, x1, g1 = (aligned[k * KIND_ROWS : (k + 1) * KIND_ROWS] for k in range(KINDS))
    up = jnp.concatenate([weights[2 * k * part : (2 * k + 1) * part] for k in range(NEAR)], axis=0)
    down = jnp.concatenate(
        [weights[(2 * k + 1) * part : (2 * k + 2) * part] for k in range(NEAR)], axis=0
    )
    act = nt(x0, up[:, :half]) + nt(x1, up[:, half:])
    back_h = nt(g0, down[:, :half]) + nt(g1, down[:, half:])
    sig = jax.nn.sigmoid(act)
    hid_ref[...] = (act * sig).astype(jnp.bfloat16)
    d_act = (back_h * sig * (1.0 + act * (1.0 - sig))).astype(jnp.bfloat16)
    da_ref[...] = d_act
    return jnp.concatenate([nn(d_act, up[:, :half]), nn(d_act, up[:, half:])], axis=0).astype(
        jnp.bfloat16
    )


def first_kernel(m_ref, w_ref, aligned_ref, da_ref, hid_ref, d_ref):
    d_ref[...] = work(m_ref[...], w_ref[...], aligned_ref, da_ref, hid_ref)


def second_kernel(m_ref, w_ref, other_ref, aligned_ref, da_ref, hid_ref, d_ref):
    mine = work(m_ref[...], w_ref[...], aligned_ref, da_ref, hid_ref)
    both = jnp.concatenate([other_ref[...], mine], axis=0)
    out, src = iota((ROWS, ROWS), 0), iota((ROWS, ROWS), 1)
    half_of, stream = (out % BLOCK) // (2 * CAP), (out // CAP) % 2
    wanted = stream * 2 * KIND_ROWS + half_of * KIND_ROWS + (out // BLOCK) * CAP + out % CAP
    d_ref[...] = nn(one_hot(src == wanted), both).astype(jnp.bfloat16)


def experts_backward(rows, weights, other=None):
    half = rows.shape[1]
    hidden = weights.shape[0] // 2
    back_rows = 2 * KIND_ROWS if other is None else ROWS
    return pl.pallas_call(
        first_kernel if other is None else second_kernel,
        out_shape=(
            jax.ShapeDtypeStruct((ROWS, half), jnp.bfloat16),
            jax.ShapeDtypeStruct((KIND_ROWS, hidden), jnp.bfloat16),
            jax.ShapeDtypeStruct((KIND_ROWS, hidden), jnp.bfloat16),
            jax.ShapeDtypeStruct((back_rows, half), jnp.bfloat16),
        ),
        in_specs=[VMEM] * (2 if other is None else 3),
        out_specs=(VMEM,) * 4,
        compiler_params=PARAMS,
        name="experts",
    )(rows, weights, *(() if other is None else (other,)))


def gradient_kernel(at_ref, la_ref, ra_ref, ld_ref, rd_ref, lh_ref, rh_ref, o_ref):
    half = la_ref.shape[1]
    hidden = ld_ref.shape[1]
    part = hidden // NEAR
    src, out = iota((hidden, 2 * hidden), 0), iota((hidden, 2 * hidden), 1)
    place = (src // part) * 2 * part + src % part
    spread = jnp.concatenate(
        [
            nn(jnp.concatenate([ld_ref[...], rd_ref[...]], axis=0), one_hot(out == place)),
            nn(jnp.concatenate([lh_ref[...], rh_ref[...]], axis=0), one_hot(out == place + part)),
        ],
        axis=0,
    ).astype(jnp.bfloat16)
    mine = at_ref[0]
    step = half // 7 if half % 7 == 0 else half
    for h in range(2):
        for start in range(0, half, step):
            cols = slice(start, start + step)
            rows = jnp.concatenate(
                [
                    ref[(2 * h + k) * KIND_ROWS : (2 * h + k + 1) * KIND_ROWS, cols]
                    for k in range(2)
                    for ref in (la_ref, ra_ref)
                ],
                axis=0,
            )
            grad = tn(rows, spread).astype(jnp.bfloat16)
            for k in range(NEAR):
                apart = mine ^ k
                slot = (apart % 2) * 2 + apart // 2
                o_ref[slot, h * half + start : h * half + start + step, :] = grad[
                    :, 2 * part * k : 2 * part * (k + 1)
                ]


def gradient(place, left, right):
    half, hidden = left[0].shape[1], left[1].shape[1]
    return pl.pallas_call(
        gradient_kernel,
        out_shape=jax.ShapeDtypeStruct((NEAR, 2 * half, 2 * hidden // NEAR), jnp.bfloat16),
        in_specs=[SMEM] + [VMEM] * 6,
        out_specs=VMEM,
        compiler_params=PARAMS,
        name="gradient",
    )(place, left[0], right[0], left[1], right[1], left[2], right[2])


def collect_kernel(m_ref, l_ref, r_ref):
    shape = (2 * BLOCK, ROWS)
    out, src = iota(shape, 0), iota(shape, 1)
    stream, half_of, expert = out // BLOCK, (out % BLOCK) // (2 * CAP), (out // CAP) % EXPERTS
    wanted = half_of * 2 * CAP + stream * CAP + out % CAP
    near = RING // EXPERTS * BLOCK
    total = nn(one_hot((src // near == expert) & (src % BLOCK == wanted)), m_ref[...])
    l_ref[...] = total[:BLOCK].astype(jnp.bfloat16)
    r_ref[...] = total[BLOCK:].astype(jnp.bfloat16)


def collect(back):
    one = jax.ShapeDtypeStruct((BLOCK, back.shape[1]), jnp.bfloat16)
    return pl.pallas_call(
        collect_kernel,
        out_shape=(one, one),
        in_specs=[VMEM],
        out_specs=(VMEM, VMEM),
        compiler_params=PARAMS,
        name="collect",
    )(back)


def finish_kernel(c_ref, e_ref, m_ref, o_ref):
    half = c_ref.shape[1] // 2
    experts = e_ref[...]
    row = iota((BLOCK, experts.shape[1]), 0)
    table = slot_table(experts, (row // CAP) % EXPERTS, row % CAP)
    for h in range(2):
        cols = slice(h * half, (h + 1) * half)
        picked = jnp.where(row // (2 * CAP) == h, table, 0.0).astype(jnp.bfloat16)
        total = c_ref[:, cols].astype(jnp.float32) + tn(picked, m_ref[...])
        o_ref[:, cols] = total.astype(jnp.bfloat16)


def finish(cot, experts, slots):
    return pl.pallas_call(
        finish_kernel,
        out_shape=jax.ShapeDtypeStruct(cot.shape, jnp.bfloat16),
        in_specs=[VMEM] * 3,
        out_specs=VMEM,
        compiler_params=PARAMS,
        name="finish",
    )(cot, experts, slots)[None]


def on_device(
    left_x,
    left_cot,
    left_experts,
    left_gates,
    right_x,
    right_cot,
    right_experts,
    right_gates,
    up_weight,
    down_weight,
):
    n_sec = lax.axis_size("section")
    n_exp = lax.axis_size("expert")
    half = left_x.shape[2] // 2
    place = lax.axis_index("expert") % NEAR
    rings = [list(range(r, n_exp, NEAR)) for r in range(NEAR)]
    chips = [list(range(z, z + NEAR)) for z in range(0, n_exp, NEAR)]

    def along_z(value):
        return lax.all_to_all(
            value, "expert", split_axis=0, concat_axis=0, tiled=True, axis_index_groups=rings
        )

    packed = jnp.concatenate([up_weight[0].T, down_weight[0].T], axis=0)
    weights = lax.all_gather(packed, "expert", axis=0, tiled=True, axis_index_groups=chips)

    copies = RING // EXPERTS
    left = prepare(left_x[0], left_cot[0], left_experts[0].T, left_gates[0].T, copies)
    right = prepare(right_x[0], right_cot[0], right_experts[0].T, right_gates[0].T, 1)
    right = send(right, "section", lambda s: n_sec - 1 - s)
    right = jnp.repeat(right.reshape(EXPERTS, 1, BLOCK, half), copies, axis=1)
    left_rows = along_z(left)
    right_rows = along_z(right.reshape(ROWS, half))

    next_cot = send(left_cot[0], "section", lambda s: s - 1)
    last_cot = send(right_cot[0], "section", lambda s: s + 1)
    next_experts = send(left_experts[0].T, "section", lambda s: s - 1)
    last_experts = send(right_experts[0].T, "section", lambda s: s + 1)

    left_work = experts_backward(left_rows, weights)
    right_work = experts_backward(right_rows, weights, left_work[3])
    back = along_z(right_work[3])

    grads = gradient(place.astype(jnp.int32)[None], left_work, right_work)
    given = send(grads[2:], "expert", lambda j: j ^ 1)
    summed = (grads[:2].astype(jnp.float32) + given.astype(jnp.float32)).astype(jnp.bfloat16)
    given = send(summed[1], "expert", lambda j: j ^ 2)
    layer_grad = (summed[0].astype(jnp.float32) + given.astype(jnp.float32)).astype(jnp.bfloat16)

    left_back, right_back = collect(back)
    next_slots = send(left_back, "section", lambda s: s - 1)
    last_slots = send(right_back, "section", lambda s: n_sec - s)
    left_grad_in = finish(next_cot, next_experts, next_slots)
    right_grad_in = finish(last_cot, last_experts, last_slots)
    return left_grad_in, right_grad_in, layer_grad[None]


def solution(mesh):
    return jax.shard_map(
        on_device,
        mesh=mesh,
        in_specs=(
            P("section", "expert", None),
            P("section", "expert", None),
            P("section", "expert", None),
            P("section", "expert", None),
            P("section", "expert", None),
            P("section", "expert", None),
            P("section", "expert", None),
            P("section", "expert", None),
            P("section", None, "expert"),
            P("section", None, "expert"),
        ),
        out_specs=(
            P("section", "expert", None),
            P("section", "expert", None),
            P("section", None, "expert"),
        ),
        check_vma=False,
    )
```

```python
import functools

import jax
import jax.numpy as jnp
from jax import lax
from jax.experimental import pallas as pl
from jax.experimental.pallas import tpu as pltpu
from jax.sharding import PartitionSpec as P

EXPERTS = 2
CAP = 6
KINDS = 4
NEAR = 4
RING = 8
BLOCK = KINDS * CAP
ROWS = RING * BLOCK
KIND_ROWS = RING * CAP
TOPK = 8
TAIL = 16
ANY = pl.BlockSpec(memory_space=pl.ANY)
VMEM = pl.BlockSpec(memory_space=pltpu.VMEM)
SMEM = pl.BlockSpec(memory_space=pltpu.SMEM)

SHORT = pl.CostEstimate(flops=1, bytes_accessed=1, transcendentals=0)


def room(mib):
    return pltpu.CompilerParams(vmem_limit_bytes=mib * 1024 * 1024)


def send(value, axis, route):
    size = lax.axis_size(axis)
    pairs = [(i, route(i)) for i in range(size)]
    return lax.ppermute(value, axis, [(a, b) for a, b in pairs if 0 <= b < size])


def iota(shape, dim):
    return lax.broadcasted_iota(jnp.int32, shape, dim)


def nn(a, b):
    return jnp.dot(a, b, preferred_element_type=jnp.float32)


def nt(a, b):
    return lax.dot_general(a, b, (((1,), (1,)), ((), ())), preferred_element_type=jnp.float32)


def tn(a, b):
    return lax.dot_general(a, b, (((0,), (0,)), ((), ())), preferred_element_type=jnp.float32)


def one_hot(mask):
    return jnp.where(mask, 1.0, 0.0).astype(jnp.bfloat16)


def slot_table(experts, expert_of, slot_of):
    tokens = experts.shape[1]
    named = [
        jnp.sum(jnp.where(experts == e, 1.0, 0.0), axis=0, keepdims=True) for e in range(EXPERTS)
    ]
    named = jnp.where(expert_of == 0, named[0], named[1])
    before = one_hot(iota((tokens, tokens), 0) < iota((tokens, tokens), 1))
    rank = nn(named.astype(jnp.bfloat16), before)
    return jnp.where(rank == slot_of.astype(jnp.float32), named, 0.0)


def spread_experts(experts, width):
    tokens = experts.shape[1]
    shape = (tokens, width)
    return nn(experts.astype(jnp.bfloat16), one_hot(iota(shape, 0) == iota(shape, 1)))


def prepare_kernel(copies, x_ref, c_ref, e_ref, g_ref, o_ref):
    half = x_ref.shape[1] // 2
    experts, gates = e_ref[...], g_ref[...]
    shape = (EXPERTS * BLOCK, experts.shape[1])
    row = iota(shape, 0)
    expert_of, kind, slot_of = row // BLOCK, (row // CAP) % KINDS, row % CAP
    table = slot_table(experts, expert_of, slot_of)
    gate = [
        jnp.sum(jnp.where(experts == e, gates, 0.0), axis=0, keepdims=True) for e in range(EXPERTS)
    ]
    gate = jnp.sum(table * jnp.where(expert_of == 0, gate[0], gate[1]), axis=1, keepdims=True)
    scale = jnp.where(kind[:, :1] % 2 == 1, gate, 1.0)
    total = None
    sources = (x_ref[:, :half], c_ref[:, :half], x_ref[:, half:], c_ref[:, half:])
    for k, source in enumerate(sources):
        part = nn(jnp.where(kind == k, table, 0.0).astype(jnp.bfloat16), source)
        total = part if total is None else total + part
    total = total * scale
    if copies == 1:
        tail = spread_experts(experts.astype(jnp.float32), half)
        tail = jnp.concatenate([tail, jnp.zeros_like(tail)], axis=0)
        o_ref[...] = jnp.concatenate([total, tail], axis=0).astype(jnp.bfloat16)
    else:
        for e in range(EXPERTS):
            one = total[e * BLOCK : (e + 1) * BLOCK].astype(jnp.bfloat16)
            two = jnp.concatenate([one, one], axis=0)
            for i in range(copies // 2):
                start = (e * copies + 2 * i) * BLOCK
                o_ref[start : start + 2 * BLOCK, :] = two


def prepare(x, cot, experts, gates, copies):
    rows = EXPERTS * copies * BLOCK + (TAIL if copies == 1 else 0)
    return pl.pallas_call(
        functools.partial(prepare_kernel, copies),
        out_shape=jax.ShapeDtypeStruct((rows, x.shape[1] // 2), jnp.bfloat16),
        in_specs=[VMEM] * 4,
        out_specs=VMEM,
        compiler_params=room(8) if copies == 1 else None,
        cost_estimate=SHORT,
        name="prepare",
    )(x, cot, experts, gates)


def align(rows):
    out, src = iota((ROWS, ROWS), 0), iota((ROWS, ROWS), 1)
    within = out % KIND_ROWS
    wanted = (within // CAP) * BLOCK + (out // KIND_ROWS) * CAP + out % CAP
    return nn(one_hot(src == wanted), rows).astype(jnp.bfloat16)


def experts_kernel(l_ref, r_ref, *refs):
    pieces, (la_ref, ra_ref, da_ref, hid_ref, o_ref, w_ref, sems) = refs[:NEAR], refs[NEAR:]
    half = l_ref.shape[1]
    hidden = w_ref.shape[0]
    part = hidden // (2 * NEAR)
    copies = [
        pltpu.make_async_copy(piece, w_ref.at[pl.ds(2 * part * k, 2 * part)], sems.at[k])
        for k, piece in enumerate(pieces)
    ]
    for copy in copies:
        copy.start()
    left, right = align(l_ref[...]), align(r_ref[...])
    la_ref[...] = left
    ra_ref[...] = right
    for copy in copies:
        copy.wait()
    both = None
    for h in range(2):
        rows = jnp.concatenate(
            [
                side[(2 * h + k) * KIND_ROWS : (2 * h + k + 1) * KIND_ROWS]
                for k in range(2)
                for side in (left, right)
            ],
            axis=0,
        )
        one = nt(rows, w_ref[:, h * half : (h + 1) * half])
        both = one if both is None else both + one
    act = both[: 2 * KIND_ROWS]
    back_h = pltpu.roll(both[2 * KIND_ROWS :], hidden - part, axis=1)
    mask = (iota(act.shape, 1) // part) % 2 == 0
    sig = jax.nn.sigmoid(act)
    hid = jnp.where(mask, act * sig, 0.0)
    hid_ref[...] = pltpu.roll(hid, part, axis=1).astype(jnp.bfloat16)
    d_act = jnp.where(mask, back_h * sig * (1.0 + act * (1.0 - sig)), 0.0).astype(jnp.bfloat16)
    da_ref[...] = d_act
    back = jnp.concatenate(
        [nn(d_act, w_ref[:, :half]), nn(d_act, w_ref[:, half:])], axis=0
    ).astype(jnp.bfloat16)
    out, src = iota((ROWS, ROWS), 0), iota((ROWS, ROWS), 1)
    half_of, stream = (out % BLOCK) // (2 * CAP), (out // CAP) % 2
    wanted = (half_of * 2 + stream) * KIND_ROWS + (out // BLOCK) * CAP + out % CAP
    o_ref[...] = nn(one_hot(src == wanted), back).astype(jnp.bfloat16)


def experts_backward(left, right, weights):
    hidden = NEAR * weights[0].shape[0]
    rows = jax.ShapeDtypeStruct(left.shape, jnp.bfloat16)
    units = jax.ShapeDtypeStruct((2 * KIND_ROWS, hidden), jnp.bfloat16)
    return pl.pallas_call(
        experts_kernel,
        out_shape=(rows, rows, units, units, rows),
        in_specs=[VMEM] * 2 + [ANY] * NEAR,
        out_specs=(VMEM,) * 5,
        scratch_shapes=[
            pltpu.VMEM((hidden, weights[0].shape[1]), jnp.bfloat16),
            pltpu.SemaphoreType.DMA((NEAR,)),
        ],
        compiler_params=room(24),
        cost_estimate=SHORT,
        name="experts",
    )(left, right, *weights)


def gradient_kernel(la_ref, ra_ref, da_ref, hid_ref, kept_ref, given_ref):
    half = la_ref.shape[1]
    width = da_ref.shape[1] // NEAR
    spread = jnp.concatenate([da_ref[...], hid_ref[...]], axis=0)
    step = half // 7 if half % 7 == 0 else half
    for h in range(2):
        for start in range(0, half, step):
            rows = jnp.concatenate(
                [
                    ref[(2 * h + k) * KIND_ROWS : (2 * h + k + 1) * KIND_ROWS, start : start + step]
                    for k in range(2)
                    for ref in (la_ref, ra_ref)
                ],
                axis=0,
            )
            grad = tn(rows, spread).astype(jnp.bfloat16)
            place = slice(h * half + start, h * half + start + step)
            for k in range(NEAR):
                ref = given_ref if k % 2 else kept_ref
                ref[k // 2, place, :] = grad[:, width * k : width * (k + 1)]


def gradient(left, right, d_act, hid):
    blocks = jax.ShapeDtypeStruct((2, 2 * left.shape[1], d_act.shape[1] // NEAR), jnp.bfloat16)
    return pl.pallas_call(
        gradient_kernel,
        out_shape=(blocks, blocks),
        in_specs=[VMEM] * 4,
        out_specs=(VMEM, VMEM),
        compiler_params=room(16),
        cost_estimate=SHORT,
        name="gradient",
    )(left, right, d_act, hid)


def add_kernel(block, *refs):
    depth = refs[-1].shape[0]
    step = depth // 4
    for i in range(4):
        rows = slice(i * step, (i + 1) * step)
        total = 0.0
        for ref in refs[:-1]:
            part = ref[block, rows, :] if len(ref.shape) == 3 else ref[rows, :]
            total = total + part.astype(jnp.float32)
        refs[-1][rows, :] = total.astype(jnp.bfloat16)


def add_blocks(block, *parts):
    return pl.pallas_call(
        functools.partial(add_kernel, block),
        out_shape=jax.ShapeDtypeStruct(parts[0].shape[1:], jnp.bfloat16),
        in_specs=[VMEM] * len(parts),
        out_specs=VMEM,
        compiler_params=room(12),
        cost_estimate=SHORT,
        name="add",
    )(*parts)


def pack_kernel(up_ref, down_ref, o_ref):
    part = up_ref.shape[0]
    o_ref[:part, :] = up_ref[...]
    o_ref[part:, :] = down_ref[...]


def pack(up, down):
    return pl.pallas_call(
        pack_kernel,
        out_shape=jax.ShapeDtypeStruct((2 * up.shape[0], up.shape[1]), jnp.bfloat16),
        in_specs=[VMEM] * 2,
        out_specs=VMEM,
        compiler_params=room(8),
        cost_estimate=SHORT,
        name="pack",
    )(up, down)


def collect_kernel(m_ref, e_ref, t_ref, l_ref, r_ref):
    shape = (2 * BLOCK, ROWS)
    out, src = iota(shape, 0), iota(shape, 1)
    stream, half_of, expert = out // BLOCK, (out % BLOCK) // (2 * CAP), (out // CAP) % EXPERTS
    wanted = half_of * 2 * CAP + stream * CAP + out % CAP
    near = RING // EXPERTS * BLOCK
    total = nn(one_hot((src // near == expert) & (src % BLOCK == wanted)), m_ref[...])
    left = spread_experts(e_ref[...].astype(jnp.float32), m_ref.shape[1])
    right = t_ref[...].astype(jnp.float32)[EXPERTS * BLOCK : EXPERTS * BLOCK + TOPK]
    l_ref[...] = jnp.concatenate([total[:BLOCK], left], axis=0).astype(jnp.bfloat16)
    r_ref[...] = jnp.concatenate([total[BLOCK:], right], axis=0).astype(jnp.bfloat16)


def collect(back, left_experts, right_message):
    one = jax.ShapeDtypeStruct((BLOCK + TOPK, back.shape[1]), jnp.bfloat16)
    return pl.pallas_call(
        collect_kernel,
        out_shape=(one, one),
        in_specs=[VMEM] * 3,
        out_specs=(VMEM, VMEM),
        compiler_params=room(8),
        cost_estimate=SHORT,
        name="collect",
    )(back, left_experts, right_message)


def finish_kernel(l_ref, r_ref, lm_ref, rm_ref, lo_ref, ro_ref, c_ref, o_ref, in_sems, out_sems):
    tokens, width = l_ref.shape
    half = width // 2
    pieces = [(side, slice(h * half, (h + 1) * half)) for side in range(2) for h in range(2)]
    arrive = [
        pltpu.make_async_copy((l_ref, r_ref)[side].at[:, cols], c_ref.at[i], in_sems.at[i])
        for i, (side, cols) in enumerate(pieces)
    ]
    leave = [
        pltpu.make_async_copy(o_ref.at[i], (lo_ref, ro_ref)[side].at[:, cols], out_sems.at[i])
        for i, (side, cols) in enumerate(pieces)
    ]
    for copy in arrive:
        copy.start()
    row = iota((BLOCK + TOPK, tokens), 0)
    for side, m_ref in enumerate((lm_ref, rm_ref)):
        experts = m_ref[:, :128].astype(jnp.float32)[BLOCK:, :tokens]
        table = slot_table(experts, (row // CAP) % EXPERTS, row % CAP)
        for h in range(2):
            picked = jnp.where(row // (2 * CAP) == h, table, 0.0).astype(jnp.bfloat16)
            added = tn(picked, m_ref[...])
            i = 2 * side + h
            arrive[i].wait()
            o_ref[i] = (c_ref[i].astype(jnp.float32) + added).astype(jnp.bfloat16)
            leave[i].start()
    for copy in leave:
        copy.wait()


def finish(left_cot, right_cot, left_slots, right_slots):
    tokens, width = left_cot.shape
    shape = jax.ShapeDtypeStruct(left_cot.shape, jnp.bfloat16)
    pieces = pltpu.VMEM((4, tokens, width // 2), jnp.bfloat16)
    return pl.pallas_call(
        finish_kernel,
        out_shape=(shape, shape),
        in_specs=[ANY] * 2 + [VMEM] * 2,
        out_specs=(ANY, ANY),
        scratch_shapes=[pieces, pieces] + [pltpu.SemaphoreType.DMA((4,))] * 2,
        compiler_params=room(12),
        cost_estimate=SHORT,
        name="finish",
    )(left_cot, right_cot, left_slots, right_slots)


def on_device(
    left_x,
    left_cot,
    left_experts,
    left_gates,
    right_x,
    right_cot,
    right_experts,
    right_gates,
    up_weight,
    down_weight,
):
    n_sec = lax.axis_size("section")
    n_exp = lax.axis_size("expert")
    half = left_x.shape[2] // 2
    rings = [list(range(r, n_exp, NEAR)) for r in range(NEAR)]

    def along_z(value):
        return lax.all_to_all(
            value, "expert", split_axis=0, concat_axis=0, tiled=True, axis_index_groups=rings
        )

    copies = RING // EXPERTS
    left = prepare(left_x[0], left_cot[0], left_experts[0].T, left_gates[0].T, copies)
    left_rows = along_z(left)
    message = prepare(right_x[0], right_cot[0], right_experts[0].T, right_gates[0].T, 1)
    message = send(message, "section", lambda s: n_sec - 1 - s)
    right = message[: EXPERTS * BLOCK].reshape(EXPERTS, 1, BLOCK, half)
    right = jnp.repeat(right, copies, axis=1).reshape(ROWS, half)

    own = pack(up_weight[0].T, down_weight[0].T)
    across = send(own, "expert", lambda j: j ^ 2)
    beside = send(own, "expert", lambda j: j ^ 1)

    next_cot = send(left_cot[0], "section", lambda s: s - 1)
    last_cot = send(right_cot[0], "section", lambda s: s + 1)
    right, left_rows = lax.optimization_barrier((right, left_rows))
    right_rows = along_z(right)
    across, next_cot = lax.optimization_barrier((across, next_cot))
    corner = send(across, "expert", lambda j: j ^ 1)

    weights = (own, beside, across, corner)
    left_rows, right_rows, d_act, hid, back = experts_backward(left_rows, right_rows, weights)
    back = along_z(back)

    kept, given = gradient(left_rows, right_rows, d_act, hid)
    given, last_cot = lax.optimization_barrier((given, last_cot))
    given = send(given, "expert", lambda j: j ^ 1)
    given_far = send(add_blocks(1, kept, given), "expert", lambda j: j ^ 2)
    layer_grad = add_blocks(0, kept, given, given_far)

    left_back, right_back = collect(back, left_experts[0].T, message)
    next_slots = send(left_back, "section", lambda s: s - 1)
    last_slots = send(right_back, "section", lambda s: n_sec - s)
    next_slots, layer_grad = lax.optimization_barrier((next_slots, layer_grad))
    left_grad_in, right_grad_in = finish(next_cot, last_cot, next_slots, last_slots)
    return left_grad_in[None], right_grad_in[None], layer_grad[None]


def solution(mesh):
    return jax.shard_map(
        on_device,
        mesh=mesh,
        in_specs=(
            P("section", "expert", None),
            P("section", "expert", None),
            P("section", "expert", None),
            P("section", "expert", None),
            P("section", "expert", None),
            P("section", "expert", None),
            P("section", "expert", None),
            P("section", "expert", None),
            P("section", None, "expert"),
            P("section", None, "expert"),
        ),
        out_specs=(
            P("section", "expert", None),
            P("section", "expert", None),
            P("section", None, "expert"),
        ),
        check_vma=False,
    )
```

```python
import functools

import jax
import jax.numpy as jnp
from jax import lax
from jax.experimental import pallas as pl
from jax.experimental.pallas import tpu as pltpu
from jax.sharding import PartitionSpec as P

EXPERTS = 2
CAP = 6
KINDS = 4
NEAR = 4
RING = 8
BLOCK = KINDS * CAP
ROWS = RING * BLOCK
KIND_ROWS = RING * CAP
PIECES = 4
TOPK = 8
ANY = pl.BlockSpec(memory_space=pl.ANY)
VMEM = pl.BlockSpec(memory_space=pltpu.VMEM)
SMEM = pl.BlockSpec(memory_space=pltpu.SMEM)

SHORT = pl.CostEstimate(flops=1, bytes_accessed=1, transcendentals=0)


def room(mib):
    return pltpu.CompilerParams(vmem_limit_bytes=mib * 1024 * 1024)


def send(value, axis, route):
    size = lax.axis_size(axis)
    pairs = [(i, route(i)) for i in range(size)]
    return lax.ppermute(value, axis, [(a, b) for a, b in pairs if 0 <= b < size])


def iota(shape, dim):
    return lax.broadcasted_iota(jnp.int32, shape, dim)


def nn(a, b):
    return jnp.dot(a, b, preferred_element_type=jnp.float32)


def nt(a, b):
    return lax.dot_general(a, b, (((1,), (1,)), ((), ())), preferred_element_type=jnp.float32)


def tn(a, b):
    return lax.dot_general(a, b, (((0,), (0,)), ((), ())), preferred_element_type=jnp.float32)


def one_hot(mask):
    return jnp.where(mask, 1.0, 0.0).astype(jnp.bfloat16)


def slot_table(experts, expert_of, slot_of):
    tokens = experts.shape[1]
    named = [
        jnp.sum(jnp.where(experts == e, 1.0, 0.0), axis=0, keepdims=True) for e in range(EXPERTS)
    ]
    named = jnp.where(expert_of == 0, named[0], named[1])
    before = one_hot(iota((tokens, tokens), 0) < iota((tokens, tokens), 1))
    rank = nn(named.astype(jnp.bfloat16), before)
    return jnp.where(rank == slot_of.astype(jnp.float32), named, 0.0)


def spread_experts(experts, width):
    tokens = experts.shape[1]
    shape = (tokens, width)
    return nn(experts.astype(jnp.bfloat16), one_hot(iota(shape, 0) == iota(shape, 1)))


def dispatch_rows(experts, gates, sources):
    shape = (EXPERTS * BLOCK, experts.shape[1])
    row = iota(shape, 0)
    expert_of, kind, slot_of = row // BLOCK, (row // CAP) % KINDS, row % CAP
    table = slot_table(experts, expert_of, slot_of)
    gate = [
        jnp.sum(jnp.where(experts == e, gates, 0.0), axis=0, keepdims=True) for e in range(EXPERTS)
    ]
    gate = jnp.sum(table * jnp.where(expert_of == 0, gate[0], gate[1]), axis=1, keepdims=True)
    scale = jnp.where(kind[:, :1] % 2 == 1, gate, 1.0)
    picks = [jnp.where(kind == k, table, 0.0).astype(jnp.bfloat16) for k in range(KINDS)]
    total = None
    for pick, source in zip(picks, sources()):
        part = nn(pick, source)
        total = part if total is None else total + part
    return (total * scale).astype(jnp.bfloat16)


def prepare_kernel(copies, x_ref, c_ref, e_ref, g_ref, o_ref):
    half = x_ref.shape[1] // 2

    def sources():
        return x_ref[:, :half], c_ref[:, :half], x_ref[:, half:], c_ref[:, half:]

    rows = dispatch_rows(e_ref[...], g_ref[...], sources)
    if copies == 1:
        o_ref[...] = rows
    else:
        for e in range(EXPERTS):
            one = rows[e * BLOCK : (e + 1) * BLOCK]
            two = jnp.concatenate([one, one], axis=0)
            for i in range(copies // 2):
                start = (e * copies + 2 * i) * BLOCK
                o_ref[start : start + 2 * BLOCK, :] = two


def prepare(x, cot, experts, gates, copies):
    return pl.pallas_call(
        functools.partial(prepare_kernel, copies),
        out_shape=jax.ShapeDtypeStruct((EXPERTS * copies * BLOCK, x.shape[1] // 2), jnp.bfloat16),
        in_specs=[VMEM] * 4,
        out_specs=VMEM,
        compiler_params=room(8) if copies == 1 else None,
        cost_estimate=SHORT,
        name="prepare",
    )(x, cot, experts, gates)


def align(rows):
    out, src = iota((ROWS, ROWS), 0), iota((ROWS, ROWS), 1)
    within = out % KIND_ROWS
    wanted = (within // CAP) * BLOCK + (out // KIND_ROWS) * CAP + out % CAP
    return nn(one_hot(src == wanted), rows).astype(jnp.bfloat16)


def experts_kernel(l_ref, r_ref, *refs):
    pieces, (la_ref, ra_ref, da_ref, hid_ref, o_ref, w_ref, sems) = refs[:NEAR], refs[NEAR:]
    half = l_ref.shape[1]
    hidden = w_ref.shape[0]
    part = hidden // (2 * NEAR)
    copies = [
        pltpu.make_async_copy(piece, w_ref.at[pl.ds(2 * part * k, 2 * part)], sems.at[k])
        for k, piece in enumerate(pieces)
    ]
    for copy in copies:
        copy.start()
    left, right = align(l_ref[...]), align(r_ref[...])
    la_ref[...] = left
    ra_ref[...] = right
    for copy in copies:
        copy.wait()
    both = None
    for h in range(2):
        rows = jnp.concatenate(
            [
                side[(2 * h + k) * KIND_ROWS : (2 * h + k + 1) * KIND_ROWS]
                for k in range(2)
                for side in (left, right)
            ],
            axis=0,
        )
        one = nt(rows, w_ref[:, h * half : (h + 1) * half])
        both = one if both is None else both + one
    act = both[: 2 * KIND_ROWS]
    back_h = pltpu.roll(both[2 * KIND_ROWS :], hidden - part, axis=1)
    mask = (iota(act.shape, 1) // part) % 2 == 0
    sig = jax.nn.sigmoid(act)
    hid = jnp.where(mask, act * sig, 0.0)
    hid_ref[...] = pltpu.roll(hid, part, axis=1).astype(jnp.bfloat16)
    d_act = jnp.where(mask, back_h * sig * (1.0 + act * (1.0 - sig)), 0.0).astype(jnp.bfloat16)
    da_ref[...] = d_act
    back = jnp.concatenate(
        [nn(d_act, w_ref[:, :half]), nn(d_act, w_ref[:, half:])], axis=0
    ).astype(jnp.bfloat16)
    out, src = iota((ROWS, ROWS), 0), iota((ROWS, ROWS), 1)
    half_of, stream = (out % BLOCK) // (2 * CAP), (out // CAP) % 2
    wanted = (half_of * 2 + stream) * KIND_ROWS + (out // BLOCK) * CAP + out % CAP
    o_ref[...] = nn(one_hot(src == wanted), back).astype(jnp.bfloat16)


def experts_backward(left, right, weights):
    hidden = NEAR * weights[0].shape[0]
    rows = jax.ShapeDtypeStruct(left.shape, jnp.bfloat16)
    units = jax.ShapeDtypeStruct((2 * KIND_ROWS, hidden), jnp.bfloat16)
    return pl.pallas_call(
        experts_kernel,
        out_shape=(rows, rows, units, units, rows),
        in_specs=[VMEM] * 2 + [ANY] * NEAR,
        out_specs=(VMEM,) * 5,
        scratch_shapes=[
            pltpu.VMEM((hidden, weights[0].shape[1]), jnp.bfloat16),
            pltpu.SemaphoreType.DMA((NEAR,)),
        ],
        compiler_params=room(48),
        cost_estimate=SHORT,
        name="experts",
    )(left, right, *weights)


def gradient_kernel(la_ref, ra_ref, da_ref, hid_ref, kept_ref, given_ref):
    half = la_ref.shape[1]
    width = da_ref.shape[1] // NEAR
    spread = jnp.concatenate([da_ref[...], hid_ref[...]], axis=0)
    step = half // 7 if half % 7 == 0 else half
    for h in range(2):
        for start in range(0, half, step):
            rows = jnp.concatenate(
                [
                    ref[(2 * h + k) * KIND_ROWS : (2 * h + k + 1) * KIND_ROWS, start : start + step]
                    for k in range(2)
                    for ref in (la_ref, ra_ref)
                ],
                axis=0,
            )
            grad = tn(rows, spread).astype(jnp.bfloat16)
            place = slice(h * half + start, h * half + start + step)
            for k in range(NEAR):
                ref = given_ref if k % 2 else kept_ref
                ref[k // 2, place, :] = grad[:, width * k : width * (k + 1)]


def gradient(left, right, d_act, hid):
    blocks = jax.ShapeDtypeStruct((2, 2 * left.shape[1], d_act.shape[1] // NEAR), jnp.bfloat16)
    return pl.pallas_call(
        gradient_kernel,
        out_shape=(blocks, blocks),
        in_specs=[VMEM] * 4,
        out_specs=(VMEM, VMEM),
        compiler_params=room(16),
        cost_estimate=SHORT,
        name="gradient",
    )(left, right, d_act, hid)


def add_kernel(a_ref, b_ref, o_ref, *, block):
    step = o_ref.shape[0] // PIECES
    for i in range(PIECES):
        rows = slice(i * step, (i + 1) * step)
        a, b = (ref[rows, :] if block is None else ref[block, rows, :] for ref in (a_ref, b_ref))
        o_ref[rows, :] = (a.astype(jnp.float32) + b.astype(jnp.float32)).astype(jnp.bfloat16)


def add_blocks(a, b, block=None):
    return pl.pallas_call(
        functools.partial(add_kernel, block=block),
        out_shape=jax.ShapeDtypeStruct(a.shape[-2:], jnp.bfloat16),
        in_specs=[VMEM] * 2,
        out_specs=VMEM,
        compiler_params=room(12),
        cost_estimate=SHORT,
        name="add",
    )(a, b)


def pack_kernel(up_ref, down_ref, o_ref):
    part = up_ref.shape[0]
    o_ref[:part, :] = up_ref[...]
    o_ref[part:, :] = down_ref[...]


def pack(up, down):
    return pl.pallas_call(
        pack_kernel,
        out_shape=jax.ShapeDtypeStruct((2 * up.shape[0], up.shape[1]), jnp.bfloat16),
        in_specs=[VMEM] * 2,
        out_specs=VMEM,
        compiler_params=room(8),
        cost_estimate=SHORT,
        name="pack",
    )(up, down)


def collect_kernel(m_ref, le_ref, re_ref, l_ref, r_ref):
    shape = (2 * BLOCK, ROWS)
    out, src = iota(shape, 0), iota(shape, 1)
    stream, half_of, expert = out // BLOCK, (out % BLOCK) // (2 * CAP), (out // CAP) % EXPERTS
    wanted = half_of * 2 * CAP + stream * CAP + out % CAP
    near = RING // EXPERTS * BLOCK
    total = nn(one_hot((src // near == expert) & (src % BLOCK == wanted)), m_ref[...])
    for i, (e_ref, o_ref) in enumerate(((le_ref, l_ref), (re_ref, r_ref))):
        table = spread_experts(e_ref[...].astype(jnp.float32), m_ref.shape[1])
        sums = total[i * BLOCK : (i + 1) * BLOCK]
        o_ref[...] = jnp.concatenate([sums, table], axis=0).astype(jnp.bfloat16)


def collect(back, left_experts, right_experts):
    one = jax.ShapeDtypeStruct((BLOCK + TOPK, back.shape[1]), jnp.bfloat16)
    return pl.pallas_call(
        collect_kernel,
        out_shape=(one, one),
        in_specs=[VMEM] * 3,
        out_specs=(VMEM, VMEM),
        compiler_params=room(8),
        cost_estimate=SHORT,
        name="collect",
    )(back, left_experts, right_experts)


def finish_kernel(l_ref, r_ref, lm_ref, rm_ref, lo_ref, ro_ref, c_ref, o_ref, in_sems, out_sems):
    tokens, width = l_ref.shape
    half = width // 2
    pieces = [(side, slice(h * half, (h + 1) * half)) for side in range(2) for h in range(2)]
    arrive = [
        pltpu.make_async_copy((l_ref, r_ref)[side].at[:, cols], c_ref.at[i], in_sems.at[i])
        for i, (side, cols) in enumerate(pieces)
    ]
    leave = [
        pltpu.make_async_copy(o_ref.at[i], (lo_ref, ro_ref)[side].at[:, cols], out_sems.at[i])
        for i, (side, cols) in enumerate(pieces)
    ]
    for copy in arrive:
        copy.start()
    row = iota((BLOCK + TOPK, tokens), 0)
    for side, m_ref in enumerate((lm_ref, rm_ref)):
        experts = m_ref[:, :128].astype(jnp.float32)[BLOCK:, :tokens]
        table = slot_table(experts, (row // CAP) % EXPERTS, row % CAP)
        for h in range(2):
            picked = jnp.where(row // (2 * CAP) == h, table, 0.0).astype(jnp.bfloat16)
            added = tn(picked, m_ref[...])
            i = 2 * side + h
            arrive[i].wait()
            o_ref[i] = (c_ref[i].astype(jnp.float32) + added).astype(jnp.bfloat16)
            leave[i].start()
    for copy in leave:
        copy.wait()


def finish(left_cot, right_cot, left_slots, right_slots):
    tokens, width = left_cot.shape
    shape = jax.ShapeDtypeStruct(left_cot.shape, jnp.bfloat16)
    pieces = pltpu.VMEM((4, tokens, width // 2), jnp.bfloat16)
    return pl.pallas_call(
        finish_kernel,
        out_shape=(shape, shape),
        in_specs=[ANY] * 2 + [VMEM] * 2,
        out_specs=(ANY, ANY),
        scratch_shapes=[pieces, pieces] + [pltpu.SemaphoreType.DMA((4,))] * 2,
        compiler_params=room(12),
        cost_estimate=SHORT,
        name="finish",
    )(left_cot, right_cot, left_slots, right_slots)


def on_device(
    left_x,
    left_cot,
    left_experts,
    left_gates,
    right_x,
    right_cot,
    right_experts,
    right_gates,
    up_weight,
    down_weight,
):
    n_sec = lax.axis_size("section")
    n_exp = lax.axis_size("expert")
    half = left_x.shape[2] // 2
    rings = [list(range(r, n_exp, NEAR)) for r in range(NEAR)]

    def along_z(value):
        return lax.all_to_all(
            value, "expert", split_axis=0, concat_axis=0, tiled=True, axis_index_groups=rings
        )

    copies = RING // EXPERTS
    left = prepare(left_x[0], left_cot[0], left_experts[0].T, left_gates[0].T, copies)
    left_rows = along_z(left)
    message = prepare(right_x[0], right_cot[0], right_experts[0].T, right_gates[0].T, 1)
    message = send(message, "section", lambda s: n_sec - 1 - s)
    mirrored = send(right_experts[0].T, "section", lambda s: n_sec - 1 - s)
    right = message.reshape(EXPERTS, 1, BLOCK, half)
    right = jnp.repeat(right, copies, axis=1).reshape(ROWS, half)

    own = pack(up_weight[0].T, down_weight[0].T)
    across = send(own, "expert", lambda j: j ^ 2)
    beside = send(own, "expert", lambda j: j ^ 1)

    next_cot = send(left_cot[0], "section", lambda s: s - 1)
    last_cot = send(right_cot[0], "section", lambda s: s + 1)
    right, left_rows = lax.optimization_barrier((right, left_rows))
    right_rows = along_z(right)
    across, next_cot, mirrored = lax.optimization_barrier((across, next_cot, mirrored))
    corner = send(across, "expert", lambda j: j ^ 1)

    weights = (own, beside, across, corner)
    left_rows, right_rows, d_act, hid, back = experts_backward(left_rows, right_rows, weights)
    back = along_z(back)

    kept, given = gradient(left_rows, right_rows, d_act, hid)
    given, last_cot = lax.optimization_barrier((given, last_cot))
    given = send(given, "expert", lambda j: j ^ 1)
    far = send(add_blocks(kept, given, 1), "expert", lambda j: j ^ 2)
    layer_grad = add_blocks(add_blocks(kept, given, 0), far)

    left_back, right_back = collect(back, left_experts[0].T, mirrored)
    next_slots = send(left_back, "section", lambda s: s - 1)
    last_slots = send(right_back, "section", lambda s: n_sec - s)
    next_slots, layer_grad = lax.optimization_barrier((next_slots, layer_grad))
    left_grad_in, right_grad_in = finish(next_cot, last_cot, next_slots, last_slots)
    return left_grad_in[None], right_grad_in[None], layer_grad[None]


def solution(mesh):
    return jax.shard_map(
        on_device,
        mesh=mesh,
        in_specs=(
            P("section", "expert", None),
            P("section", "expert", None),
            P("section", "expert", None),
            P("section", "expert", None),
            P("section", "expert", None),
            P("section", "expert", None),
            P("section", "expert", None),
            P("section", "expert", None),
            P("section", None, "expert"),
            P("section", None, "expert"),
        ),
        out_specs=(
            P("section", "expert", None),
            P("section", "expert", None),
            P("section", None, "expert"),
        ),
        check_vma=False,
    )
```

```python
import functools

import jax
import jax.numpy as jnp
from jax import lax
from jax.experimental import pallas as pl
from jax.experimental.pallas import tpu as pltpu
from jax.sharding import PartitionSpec as P

EXPERTS = 2
CAP = 6
KINDS = 4
NEAR = 4
RING = 8
BLOCK = KINDS * CAP
ROWS = RING * BLOCK
KIND_ROWS = RING * CAP
PIECES = 4
TOPK = 8
ANY = pl.BlockSpec(memory_space=pl.ANY)
VMEM = pl.BlockSpec(memory_space=pltpu.VMEM)
SMEM = pl.BlockSpec(memory_space=pltpu.SMEM)

SHORT = pl.CostEstimate(flops=1, bytes_accessed=1, transcendentals=0)


def room(mib):
    return pltpu.CompilerParams(vmem_limit_bytes=mib * 1024 * 1024)


def send(value, axis, route):
    size = lax.axis_size(axis)
    pairs = [(i, route(i)) for i in range(size)]
    return lax.ppermute(value, axis, [(a, b) for a, b in pairs if 0 <= b < size])


def iota(shape, dim):
    return lax.broadcasted_iota(jnp.int32, shape, dim)


def nn(a, b):
    return jnp.dot(a, b, preferred_element_type=jnp.float32)


def nt(a, b):
    return lax.dot_general(a, b, (((1,), (1,)), ((), ())), preferred_element_type=jnp.float32)


def tn(a, b):
    return lax.dot_general(a, b, (((0,), (0,)), ((), ())), preferred_element_type=jnp.float32)


def one_hot(mask):
    return jnp.where(mask, 1.0, 0.0).astype(jnp.bfloat16)


def slot_table(experts, expert_of, slot_of):
    tokens = experts.shape[1]
    named = [
        jnp.sum(jnp.where(experts == e, 1.0, 0.0), axis=0, keepdims=True) for e in range(EXPERTS)
    ]
    named = jnp.where(expert_of == 0, named[0], named[1])
    before = one_hot(iota((tokens, tokens), 0) < iota((tokens, tokens), 1))
    rank = nn(named.astype(jnp.bfloat16), before)
    return jnp.where(rank == slot_of.astype(jnp.float32), named, 0.0)


def spread_experts(experts, width):
    tokens = experts.shape[1]
    shape = (tokens, width)
    return nn(experts.astype(jnp.bfloat16), one_hot(iota(shape, 0) == iota(shape, 1)))


def dispatch_rows(experts, gates, sources):
    shape = (EXPERTS * BLOCK, experts.shape[1])
    row = iota(shape, 0)
    expert_of, kind, slot_of = row // BLOCK, (row // CAP) % KINDS, row % CAP
    table = slot_table(experts, expert_of, slot_of)
    gate = [
        jnp.sum(jnp.where(experts == e, gates, 0.0), axis=0, keepdims=True) for e in range(EXPERTS)
    ]
    gate = jnp.sum(table * jnp.where(expert_of == 0, gate[0], gate[1]), axis=1, keepdims=True)
    scale = jnp.where(kind[:, :1] % 2 == 1, gate, 1.0)
    picks = [jnp.where(kind == k, table, 0.0).astype(jnp.bfloat16) for k in range(KINDS)]
    total = None
    for pick, source in zip(picks, sources()):
        part = nn(pick, source)
        total = part if total is None else total + part
    return (total * scale).astype(jnp.bfloat16)


def prepare_kernel(copies, x_ref, c_ref, e_ref, g_ref, o_ref):
    half = x_ref.shape[1] // 2

    def sources():
        return x_ref[:, :half], c_ref[:, :half], x_ref[:, half:], c_ref[:, half:]

    rows = dispatch_rows(e_ref[...], g_ref[...], sources)
    if copies == 1:
        o_ref[...] = rows
    else:
        for e in range(EXPERTS):
            one = rows[e * BLOCK : (e + 1) * BLOCK]
            two = jnp.concatenate([one, one], axis=0)
            for i in range(copies // 2):
                start = (e * copies + 2 * i) * BLOCK
                o_ref[start : start + 2 * BLOCK, :] = two


def prepare(x, cot, experts, gates, copies):
    return pl.pallas_call(
        functools.partial(prepare_kernel, copies),
        out_shape=jax.ShapeDtypeStruct((EXPERTS * copies * BLOCK, x.shape[1] // 2), jnp.bfloat16),
        in_specs=[VMEM] * 4,
        out_specs=VMEM,
        compiler_params=room(8) if copies == 1 else None,
        cost_estimate=SHORT,
        name="prepare",
    )(x, cot, experts, gates)


def align(rows):
    out, src = iota((ROWS, ROWS), 0), iota((ROWS, ROWS), 1)
    within = out % KIND_ROWS
    wanted = (within // CAP) * BLOCK + (out // KIND_ROWS) * CAP + out % CAP
    return nn(one_hot(src == wanted), rows).astype(jnp.bfloat16)


def experts_kernel(l_ref, r_ref, *refs):
    pieces, (la_ref, ra_ref, da_ref, hid_ref, o_ref, w_ref, sems) = refs[:NEAR], refs[NEAR:]
    half = l_ref.shape[1]
    hidden = w_ref.shape[0]
    part = hidden // (2 * NEAR)
    copies = [
        pltpu.make_async_copy(piece, w_ref.at[pl.ds(2 * part * k, 2 * part)], sems.at[k])
        for k, piece in enumerate(pieces)
    ]
    for copy in copies:
        copy.start()
    left, right = align(l_ref[...]), align(r_ref[...])
    la_ref[...] = left
    ra_ref[...] = right
    for copy in copies:
        copy.wait()
    both = None
    for h in range(2):
        rows = jnp.concatenate(
            [
                side[(2 * h + k) * KIND_ROWS : (2 * h + k + 1) * KIND_ROWS]
                for k in range(2)
                for side in (left, right)
            ],
            axis=0,
        )
        one = nt(rows, w_ref[:, h * half : (h + 1) * half])
        both = one if both is None else both + one
    act = both[: 2 * KIND_ROWS]
    back_h = pltpu.roll(both[2 * KIND_ROWS :], hidden - part, axis=1)
    mask = (iota(act.shape, 1) // part) % 2 == 0
    sig = jax.nn.sigmoid(act)
    hid = jnp.where(mask, act * sig, 0.0)
    hid_ref[...] = pltpu.roll(hid, part, axis=1).astype(jnp.bfloat16)
    d_act = jnp.where(mask, back_h * sig * (1.0 + act * (1.0 - sig)), 0.0).astype(jnp.bfloat16)
    da_ref[...] = d_act
    back = jnp.concatenate(
        [nn(d_act, w_ref[:, :half]), nn(d_act, w_ref[:, half:])], axis=0
    ).astype(jnp.bfloat16)
    out, src = iota((ROWS, ROWS), 0), iota((ROWS, ROWS), 1)
    half_of, stream = (out % BLOCK) // (2 * CAP), (out // CAP) % 2
    wanted = (half_of * 2 + stream) * KIND_ROWS + (out // BLOCK) * CAP + out % CAP
    o_ref[...] = nn(one_hot(src == wanted), back).astype(jnp.bfloat16)


def experts_backward(left, right, weights):
    hidden = NEAR * weights[0].shape[0]
    rows = jax.ShapeDtypeStruct(left.shape, jnp.bfloat16)
    units = jax.ShapeDtypeStruct((2 * KIND_ROWS, hidden), jnp.bfloat16)
    return pl.pallas_call(
        experts_kernel,
        out_shape=(rows, rows, units, units, rows),
        in_specs=[VMEM] * 2 + [ANY] * NEAR,
        out_specs=(VMEM,) * 5,
        scratch_shapes=[
            pltpu.VMEM((hidden, weights[0].shape[1]), jnp.bfloat16),
            pltpu.SemaphoreType.DMA((NEAR,)),
        ],
        compiler_params=room(48),
        cost_estimate=SHORT,
        name="experts",
    )(left, right, *weights)


def gradient_kernel(la_ref, ra_ref, da_ref, hid_ref, kept_ref, given_ref):
    half = la_ref.shape[1]
    width = da_ref.shape[1] // NEAR
    spread = jnp.concatenate([da_ref[...], hid_ref[...]], axis=0)
    step = half // 7 if half % 7 == 0 else half
    for h in range(2):
        for start in range(0, half, step):
            rows = jnp.concatenate(
                [
                    ref[(2 * h + k) * KIND_ROWS : (2 * h + k + 1) * KIND_ROWS, start : start + step]
                    for k in range(2)
                    for ref in (la_ref, ra_ref)
                ],
                axis=0,
            )
            grad = tn(rows, spread).astype(jnp.bfloat16)
            place = slice(h * half + start, h * half + start + step)
            for k in range(NEAR):
                ref = given_ref if k % 2 else kept_ref
                ref[k // 2, place, :] = grad[:, width * k : width * (k + 1)]


def gradient(left, right, d_act, hid):
    blocks = jax.ShapeDtypeStruct((2, 2 * left.shape[1], d_act.shape[1] // NEAR), jnp.bfloat16)
    return pl.pallas_call(
        gradient_kernel,
        out_shape=(blocks, blocks),
        in_specs=[VMEM] * 4,
        out_specs=(VMEM, VMEM),
        compiler_params=room(16),
        cost_estimate=SHORT,
        name="gradient",
    )(left, right, d_act, hid)


def add_kernel(a_ref, b_ref, o_ref, in_ref=None, sems=None, *, block):
    step = o_ref.shape[0] // PIECES
    copies = []
    if block is not None:
        for i in range(PIECES):
            source = b_ref.at[block, pl.ds(i * step, step)]
            copies.append(pltpu.make_async_copy(source, in_ref.at[i], sems.at[i]))
            copies[i].start()
    for i in range(PIECES):
        rows = slice(i * step, (i + 1) * step)
        if block is None:
            a, b = a_ref[rows, :], b_ref[rows, :]
        else:
            a = a_ref[block, rows, :]
            copies[i].wait()
            b = in_ref[i]
        o_ref[rows, :] = (a.astype(jnp.float32) + b.astype(jnp.float32)).astype(jnp.bfloat16)


def add_blocks(a, b, block=None):
    depth, width = a.shape[-2:]
    scratch = [
        pltpu.VMEM((PIECES, depth // PIECES, width), jnp.bfloat16),
        pltpu.SemaphoreType.DMA((PIECES,)),
    ]
    return pl.pallas_call(
        functools.partial(add_kernel, block=block),
        out_shape=jax.ShapeDtypeStruct((depth, width), jnp.bfloat16),
        in_specs=[VMEM, VMEM if block is None else ANY],
        out_specs=VMEM,
        scratch_shapes=[] if block is None else scratch,
        compiler_params=room(12),
        cost_estimate=SHORT,
        name="add",
    )(a, b)


def pack_kernel(up_ref, down_ref, o_ref):
    part = up_ref.shape[0]
    o_ref[:part, :] = up_ref[...]
    o_ref[part:, :] = down_ref[...]


def pack(up, down):
    return pl.pallas_call(
        pack_kernel,
        out_shape=jax.ShapeDtypeStruct((2 * up.shape[0], up.shape[1]), jnp.bfloat16),
        in_specs=[VMEM] * 2,
        out_specs=VMEM,
        compiler_params=room(8),
        cost_estimate=SHORT,
        name="pack",
    )(up, down)


def collect_kernel(m_ref, le_ref, re_ref, l_ref, r_ref):
    shape = (2 * BLOCK, ROWS)
    out, src = iota(shape, 0), iota(shape, 1)
    stream, half_of, expert = out // BLOCK, (out % BLOCK) // (2 * CAP), (out // CAP) % EXPERTS
    wanted = half_of * 2 * CAP + stream * CAP + out % CAP
    near = RING // EXPERTS * BLOCK
    total = nn(one_hot((src // near == expert) & (src % BLOCK == wanted)), m_ref[...])
    for i, (e_ref, o_ref) in enumerate(((le_ref, l_ref), (re_ref, r_ref))):
        table = spread_experts(e_ref[...].astype(jnp.float32), m_ref.shape[1])
        sums = total[i * BLOCK : (i + 1) * BLOCK]
        o_ref[...] = jnp.concatenate([sums, table], axis=0).astype(jnp.bfloat16)


def collect(back, left_experts, right_experts):
    one = jax.ShapeDtypeStruct((BLOCK + TOPK, back.shape[1]), jnp.bfloat16)
    return pl.pallas_call(
        collect_kernel,
        out_shape=(one, one),
        in_specs=[VMEM] * 3,
        out_specs=(VMEM, VMEM),
        compiler_params=room(8),
        cost_estimate=SHORT,
        name="collect",
    )(back, left_experts, right_experts)


def finish_kernel(l_ref, r_ref, lm_ref, rm_ref, lo_ref, ro_ref, c_ref, o_ref, in_sems, out_sems):
    tokens, width = l_ref.shape
    half = width // 2
    pieces = [(side, slice(h * half, (h + 1) * half)) for side in range(2) for h in range(2)]
    arrive = [
        pltpu.make_async_copy((l_ref, r_ref)[side].at[:, cols], c_ref.at[i], in_sems.at[i])
        for i, (side, cols) in enumerate(pieces)
    ]
    leave = [
        pltpu.make_async_copy(o_ref.at[i], (lo_ref, ro_ref)[side].at[:, cols], out_sems.at[i])
        for i, (side, cols) in enumerate(pieces)
    ]
    for copy in arrive:
        copy.start()
    row = iota((BLOCK + TOPK, tokens), 0)
    for side, m_ref in enumerate((lm_ref, rm_ref)):
        experts = m_ref[:, :128].astype(jnp.float32)[BLOCK:, :tokens]
        table = slot_table(experts, (row // CAP) % EXPERTS, row % CAP)
        for h in range(2):
            picked = jnp.where(row // (2 * CAP) == h, table, 0.0).astype(jnp.bfloat16)
            added = tn(picked, m_ref[...])
            i = 2 * side + h
            arrive[i].wait()
            o_ref[i] = (c_ref[i].astype(jnp.float32) + added).astype(jnp.bfloat16)
            leave[i].start()
    for copy in leave:
        copy.wait()


def finish(left_cot, right_cot, left_slots, right_slots):
    tokens, width = left_cot.shape
    shape = jax.ShapeDtypeStruct(left_cot.shape, jnp.bfloat16)
    pieces = pltpu.VMEM((4, tokens, width // 2), jnp.bfloat16)
    return pl.pallas_call(
        finish_kernel,
        out_shape=(shape, shape),
        in_specs=[ANY] * 2 + [VMEM] * 2,
        out_specs=(ANY, ANY),
        scratch_shapes=[pieces, pieces] + [pltpu.SemaphoreType.DMA((4,))] * 2,
        compiler_params=room(12),
        cost_estimate=SHORT,
        name="finish",
    )(left_cot, right_cot, left_slots, right_slots)


def on_device(
    left_x,
    left_cot,
    left_experts,
    left_gates,
    right_x,
    right_cot,
    right_experts,
    right_gates,
    up_weight,
    down_weight,
):
    n_sec = lax.axis_size("section")
    n_exp = lax.axis_size("expert")
    half = left_x.shape[2] // 2
    rings = [list(range(r, n_exp, NEAR)) for r in range(NEAR)]

    def along_z(value):
        return lax.all_to_all(
            value, "expert", split_axis=0, concat_axis=0, tiled=True, axis_index_groups=rings
        )

    copies = RING // EXPERTS
    left = prepare(left_x[0], left_cot[0], left_experts[0].T, left_gates[0].T, copies)
    left_rows = along_z(left)
    message = prepare(right_x[0], right_cot[0], right_experts[0].T, right_gates[0].T, 1)
    message = send(message, "section", lambda s: n_sec - 1 - s)
    mirrored = send(right_experts[0].T, "section", lambda s: n_sec - 1 - s)
    right = message.reshape(EXPERTS, 1, BLOCK, half)
    right = jnp.repeat(right, copies, axis=1).reshape(ROWS, half)

    own = pack(up_weight[0].T, down_weight[0].T)
    across = send(own, "expert", lambda j: j ^ 2)
    beside = send(own, "expert", lambda j: j ^ 1)

    next_cot = send(left_cot[0], "section", lambda s: s - 1)
    last_cot = send(right_cot[0], "section", lambda s: s + 1)
    right, left_rows = lax.optimization_barrier((right, left_rows))
    right_rows = along_z(right)
    across, next_cot, mirrored = lax.optimization_barrier((across, next_cot, mirrored))
    corner = send(across, "expert", lambda j: j ^ 1)

    weights = (own, beside, across, corner)
    left_rows, right_rows, d_act, hid, back = experts_backward(left_rows, right_rows, weights)
    back = along_z(back)

    kept, given = gradient(left_rows, right_rows, d_act, hid)
    given, last_cot = lax.optimization_barrier((given, last_cot))
    given = send(given, "expert", lambda j: j ^ 1)
    far = send(add_blocks(kept, given, 1), "expert", lambda j: j ^ 2)
    layer_grad = add_blocks(add_blocks(kept, given, 0), far)

    left_back, right_back = collect(back, left_experts[0].T, mirrored)
    next_slots = send(left_back, "section", lambda s: s - 1)
    last_slots = send(right_back, "section", lambda s: n_sec - s)
    next_slots, layer_grad = lax.optimization_barrier((next_slots, layer_grad))
    left_grad_in, right_grad_in = finish(next_cot, last_cot, next_slots, last_slots)
    return left_grad_in[None], right_grad_in[None], layer_grad[None]


def solution(mesh):
    return jax.shard_map(
        on_device,
        mesh=mesh,
        in_specs=(
            P("section", "expert", None),
            P("section", "expert", None),
            P("section", "expert", None),
            P("section", "expert", None),
            P("section", "expert", None),
            P("section", "expert", None),
            P("section", "expert", None),
            P("section", "expert", None),
            P("section", None, "expert"),
            P("section", None, "expert"),
        ),
        out_specs=(
            P("section", "expert", None),
            P("section", "expert", None),
            P("section", None, "expert"),
        ),
        check_vma=False,
    )
```
